512 devices in a mesh: dp: 16 (over y, z_hi), tm: 32 (over z_lo, x, core).
Axes of the slice: x: 4, y: 4, z: 16 (z_hi: 4, z_lo: 4; z = z_hi * 4 + z_lo), core: 2. Of those that a mesh axis runs over, the one named last changes fastest.
Arguments:
- frames: bfloat16 [16, 24576, 1536], P('dp', 'tm')
- w_qkv: bfloat16 [1536, 2304], P('dp'), may hold values from -0.15625 to 0.15625
- utt_start: int32 [16, 24], P('dp'), may hold values from 0 to 24447, as said below
- stretch_utt: int32 [16, 96], P('dp'), may hold values from 0 to 23, as said below
- left_stretches: int32 [16, 96], P('dp'), may hold values from 0 to 2, as said below
Outputs:
- context: bfloat16 [16, 24576, 768], P('dp', 'tm')
The draws below stay inside these ranges and needn't reach their ends.
Inputs may be any that keep to these rules, and one draw needn't show every extreme that they name: `stretch_utt`: in each pack nondecreasing along blocks; utterance u covers one or more whole consecutive blocks; every utterance of 0 to 23 occurs, block 0 in utterance 0. `utt_start`: for utterance u with first block b, at least 256 * b and less than 256 * b + 128. `left_stretches`: at most the number of earlier blocks of the same utterance.
All inputs are finite; a program needn't handle non-finite values.
Results may differ from the reference program's by a relative error of at most 0.0045.
The reference program's roundings to bfloat16 on the way (of `qkv` and `probs`) count: a program that leaves them out, or rounds other values in their place, can miss the bound.
Values may be sent and summed in bfloat16 or wider, within the bound.
A program may use at most 64 MiB of HBM per device.

```python
import jax
import jax.numpy as jnp
from jax import lax

D = 1536
HEADS = 8
HEAD_DIM = 96
STRETCH = 256
LEFT = 2
HW = 768
FRAMES = 24576
NCH = 96
UTT = 24
PACKS = 16


def layout(key):

    def single(sub):
        order = jax.random.permutation(sub, NCH - 1).astype(jnp.int32)
        bounds = order[:UTT - 1] + 1
        stretch = jnp.arange(NCH, dtype=jnp.int32)
        owners = jnp.sum((bounds[None, :] <= stretch[:, None]).astype(jnp.int32), axis=1)
        ids = jnp.arange(UTT, dtype=jnp.int32)
        firsts = jnp.sum((owners[None, :] < ids[:, None]).astype(jnp.int32), axis=1)
        return (owners, firsts)
    return jax.vmap(single)(jax.random.split(key, PACKS))


def draw_frames(key, part):
    key = jax.random.fold_in(key, 3)
    return jax.random.normal(key, (PACKS, FRAMES, D), jnp.float32).astype(jnp.bfloat16)


def draw_stretch_utt(key, part):
    owners, firsts = layout(key)
    return owners


def draw_utt_start(key, part):
    owners, firsts = layout(key)
    key = jax.random.fold_in(key, 7)
    offsets = jax.random.randint(key, (PACKS, UTT), 0, STRETCH // 2, dtype=jnp.int32)
    return STRETCH * firsts + offsets


def draw_left_stretches(key, part):
    owners, firsts = layout(key)
    key = jax.random.fold_in(key, 11)
    wanted = jax.random.randint(key, (PACKS, NCH), 0, LEFT + 1, dtype=jnp.int32)
    ids = jnp.arange(UTT, dtype=jnp.int32)
    own_first = jnp.sum(jnp.where(owners[:, :, None] == ids[None, None, :], firsts[:, None, :], 0), axis=-1)
    position = jnp.arange(NCH, dtype=jnp.int32)[None, :] - own_first
    return jnp.minimum(wanted, position)


def block_levels(stream_key, shape, cuts, low, high):
    def one(axis_at, blocks):
        draws = jax.random.uniform(jax.random.fold_in(jax.random.fold_in(stream_key, 6), axis_at), (blocks,), jnp.float32, low / len(cuts), high / len(cuts))
        return jnp.repeat(jnp.exp(draws), shape[axis_at] // blocks).reshape((-1,) + (1,) * (len(shape) - axis_at - 1))

    factor_of = one(*cuts[0])
    for cut in cuts[1:]:
        factor_of = factor_of * one(*cut)
    return factor_of


def normal_values(key, extent, spread, limit, pieces=(), kind=jnp.bfloat16):
    array = jax.random.normal(key, extent, jnp.float32) * spread
    if len(pieces) > 0:
        array = block_levels(key, extent, pieces, -0.22, 0.18) * array
    return jnp.clip(array, min=-limit, max=limit).astype(kind)


def setup_inputs(seed: int = 0) -> dict:
    seeds = jax.random.split(jax.random.key(seed), 6)
    frames = draw_frames(jax.random.fold_in(seeds[5], 71), 0)
    w_qkv = normal_values(seeds[1], (D, 3 * HW), D ** -0.5, 0.15625, ((0, 16),))
    utt_start = draw_utt_start(jax.random.fold_in(seeds[5], 71), 0)
    stretch_utt = draw_stretch_utt(jax.random.fold_in(seeds[5], 71), 0)
    left_stretches = draw_left_stretches(jax.random.fold_in(seeds[5], 71), 0)
    return dict(frames=frames, w_qkv=w_qkv, utt_start=utt_start, stretch_utt=stretch_utt, left_stretches=left_stretches)


def reference(frames, w_qkv, utt_start, stretch_utt, left_stretches):
    inner = HEADS * HEAD_DIM
    reach = LEFT * STRETCH
    scale = HEAD_DIM ** -0.5

    def one_pack(pack):
        inputs, starts, owners, lefts = pack
        qkv = jnp.dot(inputs, w_qkv, preferred_element_type=jnp.float32).astype(jnp.bfloat16)
        query = qkv[:, :inner]
        keys = qkv[:, inner:2 * inner]
        values = qkv[:, 2 * inner:]
        frame = jnp.arange(inputs.shape[0], dtype=jnp.int32)
        fowner = owners[frame // STRETCH]
        live = frame >= starts[fowner]
        keys_pad = jnp.pad(keys, ((reach, 0), (0, 0)))
        values_pad = jnp.pad(values, ((reach, 0), (0, 0)))
        key_owner = jnp.concatenate([jnp.full((reach,), -1, jnp.int32), fowner])
        key_live = jnp.concatenate([jnp.zeros((reach,), bool), live])
        relative = jnp.arange(reach + STRETCH, dtype=jnp.int32) // STRETCH

        def one_stretch(block):
            start = block * STRETCH
            qblock = lax.dynamic_slice_in_dim(query, start, STRETCH, 0).astype(jnp.float32)
            kblock = lax.dynamic_slice_in_dim(keys_pad, start, reach + STRETCH, 0).astype(jnp.float32)
            vblock = lax.dynamic_slice_in_dim(values_pad, start, reach + STRETCH, 0).astype(jnp.float32)
            kown = lax.dynamic_slice_in_dim(key_owner, start, reach + STRETCH, 0)
            klive = lax.dynamic_slice_in_dim(key_live, start, reach + STRETCH, 0)
            usable = (relative >= LEFT - lefts[block]) & (kown == owners[block]) & klive
            qh = qblock.reshape(STRETCH, HEADS, HEAD_DIM)
            kh = kblock.reshape(reach + STRETCH, HEADS, HEAD_DIM)
            vh = vblock.reshape(reach + STRETCH, HEADS, HEAD_DIM)
            scores = jnp.einsum('qhd,khd->hqk', qh, kh) * scale
            scores = jnp.where(usable[None, None, :], scores, -jnp.inf)
            top = jnp.max(scores, axis=-1, keepdims=True)
            expo = jnp.exp(scores - top)
            probs = (expo / jnp.sum(expo, axis=-1, keepdims=True)).astype(jnp.bfloat16)
            probs = lax.optimization_barrier(probs).astype(jnp.float32)
            mixed = jnp.einsum('hqk,khd->qhd', probs, vh).reshape(STRETCH, inner)
            qlive = lax.dynamic_slice_in_dim(live, start, STRETCH, 0)
            return jnp.where(qlive[:, None], mixed, jnp.zeros_like(mixed)).astype(jnp.bfloat16)

        result = lax.map(one_stretch, jnp.arange(NCH, dtype=jnp.int32))
        return result.reshape(inputs.shape[0], inner)

    return lax.map(one_pack, (frames, utt_start, stretch_utt, left_stretches))
```

```python
import functools

import jax
import jax.numpy as jnp
from jax import lax
from jax.experimental import pallas as pl
from jax.experimental.pallas import tpu as pltpu
from jax.sharding import PartitionSpec as P

MESH = pl.DeviceIdType.MESH
BF16, F32 = jnp.bfloat16, jnp.float32
HEAD_DIM = 96
STRETCH = 256
ROWS = 768
CHIP = 1536
REACH = 512
DEPTH = 96
HALF = 48
COLS = 384
CHUNKS = 3
LAG = 3
SCALE = HEAD_DIM**-0.5 * 1.4426950408889634


def place():
    dp, tm = lax.axis_index("dp"), lax.axis_index("tm")
    return dp // 4, dp % 4, tm // 8, (tm // 2) % 4, tm % 2


def device(y, z, x, core):
    y, z, x = (y + 4) % 4, (z + 16) % 16, (x + 4) % 4
    return (y * 4 + z // 4, (z % 4) * 8 + x * 2 + core)


def remote(src, dst, send, recv, target):
    return pltpu.make_async_remote_copy(
        src_ref=src, dst_ref=dst, send_sem=send, recv_sem=recv, device_id=target, device_id_type=MESH
    )


def unit_at(p):
    q = p - 15
    relay = p >= 15
    chunk = jnp.where(relay, jnp.where(q < 6, q // 3, 2), p // 5)
    kind = jnp.where(relay, 5 + q % 3, p % 5)
    ok = (p >= 0) & (p < 27) & ((q < 6) | (q >= 9))
    return chunk, kind, ok


def kernel(
    x_hbm, w_hbm, start_ref, utt_ref, left_ref, out_hbm,
    xb, wb, qb, kb, vb, ob,
    lx, lw, cs, cr, hs, hr, gs, gr, zs, zr, ys, yr, bs, br, os_, or_, lo,
):
    y, zh, zl, x, core = place()
    z = zh * 4 + zl
    me = device(y, z, x, core)
    sibling = (me[0], me[1] + 1 - 2 * core)
    y_near = [device(y + d, z, x, core) for d in (1, 3, 2)]
    up, down = device(y, z + 1, x, core), device(y, z - 1, x, core)
    tm = me[1]
    chip = tm // 2
    nxt = (chip + 1) % 16
    prv = (chip + 15) % 16

    def rows_of(yy, zz, half):
        return pl.multiple_of(((yy % 4) * 4 + (zz % 4)) * DEPTH + half * HALF, 16)

    barrier = pltpu.get_barrier_semaphore()

    def greet(target):
        pl.semaphore_signal(barrier, inc=1, device_id=target, device_id_type=MESH)

    own_rows = pl.ds(rows_of(y, zh, 0), DEPTH)
    for k in range(CHUNKS):
        for j in range(3):
            col = pl.multiple_of(j * 768 + core * 384 + k * 128, 128)
            pltpu.make_async_copy(
                w_hbm.at[:, pl.ds(col, 128)], wb.at[k, own_rows, pl.ds(j * 128, 128)], lw.at[k, j]
            ).start()
    own_x = pl.ds(pl.multiple_of(REACH + core * ROWS, 16), ROWS)
    own_frames = pltpu.make_async_copy(x_hbm.at[0], xb.at[own_x], lx.at[0])
    own_frames.start()

    for t in y_near + [up, down, sibling]:
        greet(t)
    greet((me[0], prv * 2 + 1))

    @pl.when(core == 1)
    def _():
        greet((me[0], nxt * 2))
        greet((me[0], nxt * 2 + 1))

    pl.semaphore_wait(barrier, 7 + 2 * core)

    for k in range(CHUNKS):
        for j in range(3):
            pltpu.make_async_copy(
                w_hbm.at[:, pl.ds(0, 128)], wb.at[k, own_rows, pl.ds(j * 128, 128)], lw.at[k, j]
            ).wait()

    def y_own(k, i):
        part = wb.at[k, own_rows]
        return remote(part, part, ys.at[k, i], yr.at[k, i], y_near[i])

    for k in range(CHUNKS):
        for i in range(3):
            y_own(k, i).start()

    to_sibling = remote(x_hbm.at[0], xb.at[own_x], cs.at[0], cr.at[0], sibling)
    to_sibling.start()
    has_next = (core == 1) & (chip < 15)
    has_prev = chip > 0

    def halo(i):
        return remote(
            x_hbm.at[0, pl.ds(STRETCH * (i + 1), STRETCH)], xb.at[pl.ds(STRETCH * i, STRETCH)],
            hs.at[i], hr.at[0], (me[0], nxt * 2 + i),
        )

    @pl.when(has_next)
    def _():
        halo(0).start()
        halo(1).start()

    def y_own_wait(k, i):
        rows = pl.ds(rows_of(y - (1, 3, 2)[i] + 4, zh, 0), DEPTH)
        part = wb.at[k, rows]
        remote(part, part, ys.at[k, i], yr.at[k, i], y_near[i]).wait_recv()

    def unit(sign, k, kind, receiver):
        far = kind >= 5
        group = receiver - sign * jnp.where(far, 2, 1) + 8
        if sign > 0:
            off = jnp.where((kind == 2) | (kind == 7), 1, jnp.where(kind == 3, 3, jnp.where(kind == 4, 2, 0)))
        else:
            off = jnp.where(
                (kind == 2) | (kind == 6), 3, jnp.where((kind == 3) | (kind == 7), 2, jnp.where(kind == 4, 1, 0))
            )
        half = jnp.where((kind == 0) | (kind == 5), 1, 0)
        return wb.at[k, pl.ds(rows_of(y + off, group, half), HALF)], group

    def z_copy(sign, k, kind, receiver):
        part, _ = unit(sign, k, kind, receiver)
        d = (1 - sign) // 2
        n = k * 8 + kind
        return remote(part, part, zs.at[d, n], zr.at[d, n], up if sign > 0 else down)

    def used(sign, k, kind):
        even = (y + k) % 2 == 0
        return (kind != 5) | (even if sign > 0 else jnp.logical_not(even))

    def y_part(k, kind_group, i):
        part = wb.at[k, pl.ds(rows_of(y, kind_group, 1), HALF)]
        slot = (kind_group - zh + 8) % 4 - 1
        return remote(part, part, bs.at[k, slot, i], br.at[k, slot, i], y_near[i])

    def step(s):
        for sign in (1, -1):
            edge = zl == (3 if sign > 0 else 0)
            hop = zl + 1 if sign > 0 else 4 - zl
            k0, kind0, ok0 = unit_at(s)

            @pl.when(edge & ok0 & (kind0 < 5))
            def _():
                z_copy(sign, k0, kind0, zh + sign + 4).start()

            k, kind, ok = unit_at(s - hop * LAG)

            @pl.when(ok & used(sign, k, kind))
            def _():
                z_copy(sign, k, kind, zh + 4).wait_recv()

                @pl.when(jnp.logical_not(edge))
                def _():
                    z_copy(sign, k, kind, zh + 4).start()

                if sign > 0:
                    relays, relay = kind <= 2, kind + 5
                else:
                    relays = (kind == 0) | (kind == 2) | (kind == 3)
                    relay = jnp.where(kind == 0, 5, kind + 4)

                @pl.when(edge & relays & used(sign, k, relay))
                def _():
                    z_copy(sign, k, relay, zh + sign + 4).start()

                @pl.when((kind == 0) | (kind == 5))
                def _():
                    group = (zh - sign * jnp.where(kind == 5, 2, 1) + 8) % 4
                    for i in range(3):
                        y_part(k, group, i).start()

    for k in range(CHUNKS):
        for i in range(3):
            y_own_wait(k, i)

    @pl.loop(0, 27 + 4 * LAG)
    def _(s):
        step(s)

    @pl.when(has_prev)
    def _():
        part = xb.at[pl.ds(pl.multiple_of(STRETCH * core, 16), STRETCH)]
        remote(part, part, gs.at[0], hr.at[0], sibling).wait_recv()
        remote(part, part, gs.at[0], gr.at[0], sibling).start()

    @pl.when(jnp.logical_not(has_prev))
    def _():
        xb[0:REACH] = jnp.zeros((REACH, xb.shape[1]), BF16)

    own_frames.wait()
    other_x = xb.at[pl.ds(pl.multiple_of(REACH + (1 - core) * ROWS, 16), ROWS)]
    remote(other_x, other_x, cs.at[0], cr.at[0], sibling).wait_recv()

    for k in range(CHUNKS):
        for slot in range(3):
            for i in range(3):
                part = wb.at[k, pl.ds(rows_of(y - (1, 3, 2)[i] + 4, zh + slot + 1, 1), HALF)]
                remote(part, part, bs.at[k, slot, i], br.at[k, slot, i], y_near[i]).wait_recv()

    @pl.when(has_prev)
    def _():
        part = xb.at[pl.ds(pl.multiple_of(STRETCH * (1 - core), 16), STRETCH)]
        remote(part, part, gs.at[0], gr.at[0], sibling).wait_recv()

    @pl.loop(0, 8)
    def _(r):
        rr = pl.ds(pl.multiple_of(r * STRETCH, STRETCH), STRETCH)
        a = xb[rr, :]
        for k in range(CHUNKS):
            p = jnp.dot(a, wb[k], preferred_element_type=F32).astype(BF16)
            to = slice(k * 128, (k + 1) * 128)
            qb[rr, to] = p[:, 0:128]
            kb[rr, to] = p[:, 128:256]
            vb[rr, to] = p[:, 256:384]

    lane = lax.broadcasted_iota(jnp.int32, (1, 128), 1)

    def attend(h, b, bias):
        t0, t1 = (h * HEAD_DIM) // 128, (h * HEAD_DIM + HEAD_DIM - 1) // 128
        width = (t1 - t0 + 1) * 128
        low = h * HEAD_DIM - t0 * 128
        lanes = lax.broadcasted_iota(jnp.int32, (1, width), 1)
        mine = (lanes >= low) & (lanes < low + HEAD_DIM)
        rq = pl.ds(pl.multiple_of((b + 2) * STRETCH, STRETCH), STRETCH)
        rk = pl.ds(pl.multiple_of(b * STRETCH, STRETCH), 3 * STRETCH)
        cols = slice(t0 * 128, t0 * 128 + width)
        q = jnp.where(mine, qb[rq, cols], jnp.zeros((), BF16))
        v = jnp.where(mine, vb[rk, cols], jnp.ones((), BF16))
        s = lax.dot_general(q, kb[rk, cols], (((1,), (1,)), ((), ())), preferred_element_type=F32)
        s = s + bias
        m = jnp.max(s, axis=1, keepdims=True)
        e = jnp.exp2((s - m) * SCALE).astype(BF16)
        o = jnp.dot(e, v, preferred_element_type=F32)
        one = 0 if low > 0 else HEAD_DIM
        return o / o[:, one : one + 1]

    def out_local(b, to):
        rr = pl.ds(pl.multiple_of(b * STRETCH, STRETCH), STRETCH)
        ro = pl.ds(pl.multiple_of(to * STRETCH, STRETCH), STRETCH)
        mine = out_hbm.at[0, ro, pl.ds(pl.multiple_of(core * COLS, 128), COLS)]
        return rr, mine

    @pl.loop(0, 6)
    def _(b):
        block = chip * 6 + b
        owner = utt_ref[0, block]
        reach = left_ref[0, block]
        start = start_ref[0, owner]
        parts = []
        for d in (2, 1, 0):
            j = block - d
            ok = (j >= 0) & (utt_ref[0, jnp.maximum(j, 0)] == owner) & (reach >= d)
            pos = j * STRETCH + lax.broadcasted_iota(jnp.int32, (1, STRETCH), 1)
            first = jnp.where(ok, start, 1 << 30)
            parts.append(jnp.where(pos >= first, 0.0, -jnp.inf).astype(F32))
        bias = jnp.concatenate(parts, axis=1)
        live = block * STRETCH + lax.broadcasted_iota(jnp.int32, (STRETCH, 1), 0) >= start
        o0, o1, o2, o3 = [attend(h, b, bias) for h in range(4)]
        rr = pl.ds(pl.multiple_of(b * STRETCH, STRETCH), STRETCH)
        zero = jnp.zeros((), F32)
        ob[rr, 0:128] = jnp.where(live, jnp.where(lane < 96, o0, o1[:, :128]), zero).astype(BF16)
        ob[rr, 128:256] = jnp.where(live, jnp.where(lane < 64, o1[:, 128:], o2[:, :128]), zero).astype(BF16)
        ob[rr, 256:384] = jnp.where(live, jnp.where(lane < 32, o2[:, 128:], o3), zero).astype(BF16)
        i = b % 3
        src, dst = out_local(b, i)
        here = (b // 3) == core

        @pl.when(here)
        def _():
            pltpu.make_async_copy(ob.at[src], dst, lo.at[i]).start()

        @pl.when(jnp.logical_not(here))
        def _():
            remote(ob.at[src], dst, os_.at[i], or_.at[i], sibling).start()

    for i in range(3):
        src, dst = out_local(i, i)
        pltpu.make_async_copy(ob.at[src], dst, lo.at[i]).wait()
        other = out_hbm.at[0, pl.ds(i * STRETCH, STRETCH), pl.ds(pl.multiple_of((1 - core) * COLS, 128), COLS)]
        c = remote(ob.at[src], other, os_.at[i], or_.at[i], sibling)
        c.wait_send()
        c.wait_recv()
    for k in range(CHUNKS):
        for i in range(3):
            y_own(k, i).wait_send()
        for slot in range(3):
            for i in range(3):
                part = wb.at[k, pl.ds(0, HALF)]
                remote(part, part, bs.at[k, slot, i], br.at[k, slot, i], y_near[i]).wait_send()
        for sign in (1, -1):
            for kind in range(8):

                def drain(sign=sign, k=k, kind=kind):
                    z_copy(sign, k, kind, zh + 4).wait_send()

                if kind == 5:
                    pl.when(used(sign, k, kind))(drain)
                else:
                    drain()
    to_sibling.wait_send()

    @pl.when(has_next)
    def _():
        halo(0).wait_send()
        halo(1).wait_send()

    @pl.when(has_prev)
    def _():
        part = xb.at[pl.ds(pl.multiple_of(STRETCH * core, 16), STRETCH)]
        remote(part, part, gs.at[0], gr.at[0], sibling).wait_send()


def local(frames, w_qkv, utt_start, stretch_utt, left_stretches):
    any_ = pl.BlockSpec(memory_space=pl.ANY)
    smem = pl.BlockSpec(memory_space=pltpu.SMEM)
    dma = pltpu.SemaphoreType.DMA
    return pl.pallas_call(
        kernel,
        out_shape=jax.ShapeDtypeStruct((1, ROWS, 768), BF16),
        in_specs=[any_, any_, smem, smem, smem],
        out_specs=any_,
        scratch_shapes=[
            pltpu.VMEM((REACH + CHIP, 1536), BF16),
            pltpu.VMEM((CHUNKS, 1536, COLS), BF16),
            pltpu.VMEM((REACH + CHIP, COLS), BF16),
            pltpu.VMEM((REACH + CHIP, COLS), BF16),
            pltpu.VMEM((REACH + CHIP, COLS), BF16),
            pltpu.VMEM((CHIP, COLS), BF16),
            dma((1,)), dma((CHUNKS, 3)),
            dma((1,)), dma((1,)), dma((2,)), dma((1,)), dma((1,)), dma((1,)),
            dma((2, 24)), dma((2, 24)), dma((CHUNKS, 3)), dma((CHUNKS, 3)),
            dma((CHUNKS, 3, 3)), dma((CHUNKS, 3, 3)),
            dma((3,)), dma((3,)), dma((3,)),
        ],
        compiler_params=pltpu.CompilerParams(
            collective_id=0, has_side_effects=True, vmem_limit_bytes=60 << 20
        ),
        name="block_attention",
    )(frames, w_qkv, utt_start, stretch_utt, left_stretches)


def solution(mesh):
    return jax.shard_map(
        local,
        mesh=mesh,
        in_specs=(P("dp", "tm", None), P("dp", None), P("dp", None), P("dp", None), P("dp", None)),
        out_specs=P("dp", "tm", None),
        check_vma=False,
    )
```

```python
import functools

import jax
import jax.numpy as jnp
from jax import lax
from jax.experimental import pallas as pl
from jax.experimental.pallas import tpu as pltpu
from jax.sharding import PartitionSpec as P

MESH = pl.DeviceIdType.MESH
BF16, F32 = jnp.bfloat16, jnp.float32
HEAD_DIM = 96
STRETCH = 256
ROWS = 768
CHIP = 1536
REACH = 512
DEPTH = 96
HALF = 48
PART = 32
COLS = 384
CHUNKS = 3
SCALE = HEAD_DIM**-0.5 * 1.4426950408889634


def place():
    dp, tm = lax.axis_index("dp"), lax.axis_index("tm")
    return dp // 4, dp % 4, tm // 8, (tm // 2) % 4, tm % 2


def device(y, z, x, core):
    y, z, x = (y + 4) % 4, (z + 16) % 16, (x + 4) % 4
    return (y * 4 + z // 4, (z % 4) * 8 + x * 2 + core)


def remote(src, dst, send, recv, target):
    return pltpu.make_async_remote_copy(
        src_ref=src, dst_ref=dst, send_sem=send, recv_sem=recv, device_id=target, device_id_type=MESH
    )


def kernel(
    x_hbm, w_hbm, start_ref, utt_ref, left_ref, out_hbm,
    xb, wb, qb, kb, vb, ob, masks, acc,
    lx, lw, cs, cr, hs, hr, gs, gr, zs, zr, xs, xr, ys, yr, fs, fr, os_, or_, lo, ready,
):
    y, zh, zl, x, core = place()
    z = zh * 4 + zl
    me = device(y, z, x, core)
    sibling = (me[0], me[1] + 1 - 2 * core)
    y_to = [device(y + 1, z, x, core), device(y + 3, z, x, core)]
    others = [jnp.where(zh == 3, 2 - j, j + jnp.where(j >= zh, 1, 0)) for j in range(3)]
    z_to = [device(y, o * 4 + zl, x, core) for o in others]
    x_to = [device(y, z, x + d, core) for d in (1, 2, 3)]
    groups = [zh] + others
    chip = me[1] // 2
    nxt, prv = (chip + 1) % 16, (chip + 15) % 16

    def rows_of(yy, e, start, count):
        first = ((yy + 4) % 4 * 4 + groups[e]) * DEPTH + start
        return pl.ds(pl.multiple_of(first, 16), count)

    barrier = pltpu.get_barrier_semaphore()

    def greet(target):
        pl.semaphore_signal(barrier, inc=1, device_id=target, device_id_type=MESH)

    own_rows = rows_of(y, 0, 0, DEPTH)

    def own_weights(k, j):
        col = pl.multiple_of(j * 768 + core * 384 + k * 128, 128)
        return pltpu.make_async_copy(
            w_hbm.at[:, pl.ds(col, 128)], wb.at[k, own_rows, pl.ds(j * 128, 128)], lw.at[k, j]
        )

    for k in range(CHUNKS):
        for j in range(3):
            own_weights(k, j).start()
    own_x = pl.ds(pl.multiple_of(REACH + core * ROWS, 16), ROWS)
    own_frames = pltpu.make_async_copy(x_hbm.at[0], xb.at[own_x], lx.at[0])
    own_frames.start()

    has_next = (core == 1) & (chip < 15)
    has_prev = chip > 0
    for t in y_to + x_to + [sibling]:
        greet(t)

    for j in range(3):

        @pl.when((x < 3) & (others[j] > zh))
        def _():
            greet(z_to[j])

    @pl.when(has_prev)
    def _():
        greet((me[0], prv * 2 + 1))

    @pl.when(has_next)
    def _():
        greet((me[0], nxt * 2))
        greet((me[0], nxt * 2 + 1))

    peers = 6 + jnp.where(x < 3, zh, 0) + jnp.where(has_prev, 1, 0) + jnp.where(has_next, 2, 0)
    pl.semaphore_wait(barrier, peers)

    for j in range(3):

        @pl.when((x < 3) & (others[j] < zh))
        def _():
            pl.semaphore_signal(ready.at[zh], inc=1, device_id=z_to[j], device_id_type=MESH)

    def z_copy(k, j, e, source):
        part = wb.at[k, rows_of(y, e, PART * jnp.minimum(x, 2), PART)]
        return remote(part, part, zs.at[k, j], zr.at[k, source], z_to[j])

    def x_copy(k, i, d, owner):
        part = wb.at[k, rows_of(y, i + 1, PART * jnp.minimum(owner, 2), PART)]
        return remote(part, part, xs.at[k, i, d], xr.at[k, i, d], x_to[d])

    def y_copy(k, e, d, yy):
        part = wb.at[k, rows_of(yy, e, 0, DEPTH)]
        return remote(part, part, ys.at[k, e, d], yr.at[k, e, d], y_to[d])

    def f_copy(k, e, d, yy):
        part = wb.at[k, rows_of(yy, e, HALF * d, HALF)]
        return remote(part, part, fs.at[k, e, d], fr.at[k, e, d], y_to[d])

    def z_send(j):
        for k in range(CHUNKS):
            z_copy(k, j, 0, zh).start()

    def z_down():
        for j in range(3):

            @pl.when((x < 3) & (others[j] < zh))
            def _():
                z_send(j)

    def z_up(j):
        @pl.when((x < 3) & (others[j] > zh))
        def _():
            pl.semaphore_wait(ready.at[others[j]], 1)
            z_send(j)

    def y_send(k, e):
        for d in range(2):
            y_copy(k, e, d, y).start()

    def z_to_x(k, j):
        @pl.when(x < 3)
        def _():
            z_copy(k, j, j + 1, others[j]).wait_recv()
            for d in range(3):
                x_copy(k, j, d, x).start()

    def x_to_y(k, j):
        for d in range(3):
            owner = (x + 3 - d) % 4

            @pl.when(owner < 3)
            def _():
                x_copy(k, j, d, owner).wait_recv()

        y_send(k, j + 1)

    def y_to_f(k, e):
        for d in range(2):
            yy = y + (3, 1)[d]
            y_copy(k, e, d, yy).wait_recv()
            f_copy(k, e, d, yy).start()

    def f_end(k, e):
        for d in range(2):
            f_copy(k, e, d, y + 2).wait_recv()

    def halo(i):
        return remote(
            x_hbm.at[0, pl.ds(STRETCH * (i + 1), STRETCH)], xb.at[pl.ds(STRETCH * i, STRETCH)],
            hs.at[i], hr.at[0], (me[0], nxt * 2 + i),
        )

    def halo_across(part_of):
        part = xb.at[pl.ds(pl.multiple_of(STRETCH * part_of, 16), STRETCH)]
        return remote(part, part, gs.at[0], gr.at[0], sibling)

    def to_sibling(rows):
        part = xb.at[pl.ds(pl.multiple_of(REACH + rows * ROWS, 16), ROWS)]
        return remote(x_hbm.at[0], part, cs.at[0], cr.at[0], sibling)

    for k in range(CHUNKS):
        for j in range(3):
            own_weights(k, j).wait()
        y_send(k, 0)
    z_down()
    to_sibling(core).start()

    @pl.when(has_next)
    def _():
        halo(0).start()
        halo(1).start()

    @pl.loop(0, 6)
    def _(b):
        block = chip * 6 + b
        owner = utt_ref[0, block]
        reach = left_ref[0, block]
        start = start_ref[0, owner]
        for d in (2, 1, 0):
            j = block - d
            ok = (j >= 0) & (utt_ref[0, jnp.maximum(j, 0)] == owner) & (reach >= d)
            pos = j * STRETCH + lax.broadcasted_iota(jnp.int32, (1, STRETCH), 1)
            first = jnp.where(ok, start, 1 << 30)
            at = STRETCH * (2 - d)
            masks[pl.ds(b, 1), at : at + STRETCH] = jnp.where(pos >= first, 0.0, -jnp.inf).astype(F32)

    @pl.when(jnp.logical_not(has_prev))
    def _():
        xb[0:REACH] = jnp.zeros((REACH, xb.shape[1]), BF16)

    late = pl.multiple_of(jnp.where(zh == 3, 0, 256), 128)
    soon = pl.multiple_of(256 - late, 128)

    def tiles(ref, k, rr, at):
        if k is None:
            return [ref[rr, pl.ds(pl.multiple_of(yy * 384 + at, 128), 128)] for yy in range(4)]
        return [ref[k, pl.ds(pl.multiple_of(yy * 384 + at, 128), 128), :] for yy in range(4)]

    def project_soon(k, lo_, hi):
        @pl.loop(lo_, hi)
        def _(r):
            rr = pl.ds(pl.multiple_of(r * STRETCH, STRETCH), STRETCH)
            xs_ = jnp.concatenate(tiles(xb, None, rr, 128) + tiles(xb, None, rr, soon), axis=1)
            ws_ = jnp.concatenate(tiles(wb, k, rr, 128) + tiles(wb, k, rr, soon), axis=0)
            acc[k, rr, :] = jnp.dot(xs_, ws_, preferred_element_type=F32)

    def project(k, lo_, hi):
        @pl.loop(lo_, hi)
        def _(r):
            rr = pl.ds(pl.multiple_of(r * STRETCH, STRETCH), STRETCH)
            xs_ = jnp.concatenate(tiles(xb, None, rr, late), axis=1)
            ws_ = jnp.concatenate(tiles(wb, k, rr, late), axis=0)
            p = (acc[k, rr, :] + jnp.dot(xs_, ws_, preferred_element_type=F32)).astype(BF16)
            to = slice(k * 128, (k + 1) * 128)
            qb[rr, to] = p[:, 0:128]
            kb[rr, to] = p[:, 128:256]
            vb[rr, to] = p[:, 256:384]

    lane = lax.broadcasted_iota(jnp.int32, (1, 128), 1)

    def window(h):
        t0, t1 = (h * HEAD_DIM) // 128, (h * HEAD_DIM + HEAD_DIM - 1) // 128
        low, width = h * HEAD_DIM - t0 * 128, (t1 - t0 + 1) * 128
        lanes = lax.broadcasted_iota(jnp.int32, (1, width), 1)
        return slice(t0 * 128, t0 * 128 + width), low, (lanes >= low) & (lanes < low + HEAD_DIM)

    def scores_of(h, b):
        cols, _, mine = window(h)
        rq = pl.ds(pl.multiple_of((b + 2) * STRETCH, STRETCH), STRETCH)
        rk = pl.ds(pl.multiple_of(b * STRETCH, STRETCH), 3 * STRETCH)
        q = jnp.where(mine, qb[rq, cols], jnp.zeros((), BF16))
        return lax.dot_general(q, kb[rk, cols], (((1,), (1,)), ((), ())), preferred_element_type=F32)

    def weights_of(s, bias):
        s = s + bias
        return jnp.exp2((s - jnp.max(s, axis=1, keepdims=True)) * SCALE).astype(BF16)

    def mixed_of(h, b, e, live):
        cols, low, mine = window(h)
        rk = pl.ds(pl.multiple_of(b * STRETCH, STRETCH), 3 * STRETCH)
        v = jnp.where(mine, vb[rk, cols], jnp.ones((), BF16))
        o = jnp.dot(e, v, preferred_element_type=F32)
        one = 0 if low > 0 else HEAD_DIM
        return jnp.where(live, o / o[:, one : one + 1], 0.0).astype(BF16)

    def block_of(b):
        block = chip * 6 + b
        start = start_ref[0, utt_ref[0, block]]
        live = block * STRETCH + lax.broadcasted_iota(jnp.int32, (STRETCH, 1), 0) >= start
        rr = pl.ds(pl.multiple_of(b * STRETCH, STRETCH), STRETCH)
        return live, rr, masks[pl.ds(b, 1), :]

    def out_parts(b, to):
        src = pl.ds(pl.multiple_of(b * STRETCH, STRETCH), STRETCH)
        ro = pl.ds(pl.multiple_of(to * STRETCH, STRETCH), STRETCH)
        return src, out_hbm.at[0, ro, pl.ds(pl.multiple_of(core * COLS, 128), COLS)]

    def attend(lo_, hi):
        @pl.loop(lo_, hi)
        def _(b):
            live, rr, bias = block_of(b)
            heads = range(4)
            scores = [scores_of(h, b) for h in heads]
            shares = [weights_of(s, bias) for s in scores]
            o = [mixed_of(h, b, shares[h], live) for h in heads]
            ob[rr, 0:128] = jnp.where(lane < 96, o[0], o[1][:, :128])
            ob[rr, 128:256] = jnp.where(lane < 64, o[1][:, 128:], o[2][:, :128])
            ob[rr, 256:384] = jnp.where(lane < 32, o[2][:, 128:], o[3])
            i = b % 3
            src, dst = out_parts(b, i)
            here = (b // 3) == core

            @pl.when(here)
            def _():
                pltpu.make_async_copy(ob.at[src], dst, lo.at[i]).start()

            @pl.when(jnp.logical_not(here))
            def _():
                remote(ob.at[src], dst, os_.at[i], or_.at[i], sibling).start()

    z_up(0)
    for k in range(CHUNKS):
        y_to_f(k, 0)
    z_up(1)
    z_up(2)
    for k in range(CHUNKS):
        z_to_x(k, 0)
        z_to_x(k, 1)
    for k in range(CHUNKS):
        x_to_y(k, 0)
        x_to_y(k, 1)
    for k in range(CHUNKS):
        z_to_x(k, 2)
    for k in range(CHUNKS):
        y_to_f(k, 1)
        y_to_f(k, 2)
    for k in range(CHUNKS):
        x_to_y(k, 2)
    own_frames.wait()
    to_sibling(1 - core).wait_recv()
    for k in range(CHUNKS):
        for e in range(3):
            f_end(k, e)
        project_soon(k, 2, 5)
        y_to_f(k, 3)
        project_soon(k, 5, 8)

    @pl.when(has_prev)
    def _():
        part = xb.at[pl.ds(pl.multiple_of(STRETCH * core, 16), STRETCH)]
        remote(part, part, gs.at[0], hr.at[0], sibling).wait_recv()
        halo_across(core).start()

    for k in range(CHUNKS):
        f_end(k, 3)
        project(k, 2, 8)

    @pl.when(has_prev)
    def _():
        halo_across(1 - core).wait_recv()

    for k in range(CHUNKS):
        project_soon(k, 0, 2)
        project(k, 0, 2)
    attend(0, 6)

    for i in range(3):
        src, dst = out_parts(i, i)
        pltpu.make_async_copy(ob.at[src], dst, lo.at[i]).wait()
        other = out_hbm.at[0, pl.ds(i * STRETCH, STRETCH), pl.ds(pl.multiple_of((1 - core) * COLS, 128), COLS)]
        c = remote(ob.at[src], other, os_.at[i], or_.at[i], sibling)
        c.wait_send()
        c.wait_recv()
    for k in range(CHUNKS):
        for e in range(4):
            for d in range(2):
                y_copy(k, e, d, y).wait_send()
                f_copy(k, e, d, y).wait_send()

        @pl.when(x < 3)
        def _():
            for i in range(3):
                z_copy(k, i, 0, zh).wait_send()
                for d in range(3):
                    x_copy(k, i, d, x).wait_send()

    to_sibling(core).wait_send()

    @pl.when(has_next)
    def _():
        halo(0).wait_send()
        halo(1).wait_send()

    @pl.when(has_prev)
    def _():
        halo_across(core).wait_send()


def local(frames, w_qkv, utt_start, stretch_utt, left_stretches):
    any_ = pl.BlockSpec(memory_space=pl.ANY)
    smem = pl.BlockSpec(memory_space=pltpu.SMEM)
    dma = pltpu.SemaphoreType.DMA
    return pl.pallas_call(
        kernel,
        out_shape=jax.ShapeDtypeStruct((1, ROWS, 768), BF16),
        in_specs=[any_, any_, smem, smem, smem],
        out_specs=any_,
        scratch_shapes=[
            pltpu.VMEM((REACH + CHIP, 1536), BF16),
            pltpu.VMEM((CHUNKS, 1536, COLS), BF16),
            pltpu.VMEM((REACH + CHIP, COLS), BF16),
            pltpu.VMEM((REACH + CHIP, COLS), BF16),
            pltpu.VMEM((REACH + CHIP, COLS), BF16),
            pltpu.VMEM((CHIP, COLS), BF16),
            pltpu.VMEM((8, 3 * STRETCH), F32),
            pltpu.VMEM((CHUNKS, REACH + CHIP, COLS), F32),
            dma((1,)), dma((CHUNKS, 3)),
            dma((1,)), dma((1,)), dma((2,)), dma((1,)), dma((1,)), dma((1,)),
            dma((CHUNKS, 3)), dma((CHUNKS, 4)), dma((CHUNKS, 3, 3)), dma((CHUNKS, 3, 3)),
            dma((CHUNKS, 4, 2)), dma((CHUNKS, 4, 2)), dma((CHUNKS, 4, 2)), dma((CHUNKS, 4, 2)),
            dma((3,)), dma((3,)), dma((3,)),
            pltpu.SemaphoreType.REGULAR((4,)),
        ],
        compiler_params=pltpu.CompilerParams(
            collective_id=0, has_side_effects=True, vmem_limit_bytes=60 << 20
        ),
        name="block_attention",
    )(frames, w_qkv, utt_start, stretch_utt, left_stretches)


def solution(mesh):
    return jax.shard_map(
        local,
        mesh=mesh,
        in_specs=(P("dp", "tm", None), P("dp", None), P("dp", None), P("dp", None), P("dp", None)),
        out_specs=P("dp", "tm", None),
        check_vma=False,
    )
```

```python
import functools

import jax
import jax.numpy as jnp
from jax import lax
from jax.experimental import pallas as pl
from jax.experimental.pallas import tpu as pltpu
from jax.sharding import PartitionSpec as P

MESH = pl.DeviceIdType.MESH
BF16, F32 = jnp.bfloat16, jnp.float32
HEAD_DIM = 96
STRETCH = 256
ROWS = 768
CHIP = 1536
REACH = 512
DEPTH = 96
HALF = 48
PART = 32
COLS = 384
CHUNKS = 3
SCALE = HEAD_DIM**-0.5 * 1.4426950408889634


def place():
    dp, tm = lax.axis_index("dp"), lax.axis_index("tm")
    return dp // 4, dp % 4, tm // 8, (tm // 2) % 4, tm % 2


def device(y, z, x, core):
    y, z, x = (y + 4) % 4, (z + 16) % 16, (x + 4) % 4
    return (y * 4 + z // 4, (z % 4) * 8 + x * 2 + core)


def remote(src, dst, send, recv, target):
    return pltpu.make_async_remote_copy(
        src_ref=src, dst_ref=dst, send_sem=send, recv_sem=recv, device_id=target, device_id_type=MESH
    )


def kernel(
    x_hbm, w_hbm, start_ref, utt_ref, left_ref, out_hbm,
    xb, wb, qb, kb, vb, ob, masks,
    lx, lw, cs, cr, hs, hr, gs, gr, zs, zr, xs, xr, ys, yr, fs, fr, os_, or_, lo, ready,
):
    y, zh, zl, x, core = place()
    z = zh * 4 + zl
    me = device(y, z, x, core)
    sibling = (me[0], me[1] + 1 - 2 * core)
    y_to = [device(y + 1, z, x, core), device(y + 3, z, x, core)]
    others = [jnp.where(zh == 3, 2 - j, j + jnp.where(j >= zh, 1, 0)) for j in range(3)]
    z_to = [device(y, o * 4 + zl, x, core) for o in others]
    x_to = [device(y, z, x + d, core) for d in (1, 2, 3)]
    groups = [zh] + others
    chip = me[1] // 2
    nxt, prv = (chip + 1) % 16, (chip + 15) % 16

    def rows_of(yy, e, start, count):
        first = ((yy + 4) % 4 * 4 + groups[e]) * DEPTH + start
        return pl.ds(pl.multiple_of(first, 16), count)

    barrier = pltpu.get_barrier_semaphore()

    def greet(target):
        pl.semaphore_signal(barrier, inc=1, device_id=target, device_id_type=MESH)

    own_rows = rows_of(y, 0, 0, DEPTH)

    def own_weights(k, j):
        col = pl.multiple_of(j * 768 + core * 384 + k * 128, 128)
        return pltpu.make_async_copy(
            w_hbm.at[:, pl.ds(col, 128)], wb.at[k, own_rows, pl.ds(j * 128, 128)], lw.at[k, j]
        )

    for k in range(CHUNKS):
        for j in range(3):
            own_weights(k, j).start()
    own_x = pl.ds(pl.multiple_of(REACH + core * ROWS, 16), ROWS)
    own_frames = pltpu.make_async_copy(x_hbm.at[0], xb.at[own_x], lx.at[0])
    own_frames.start()

    has_next = (core == 1) & (chip < 15)
    has_prev = chip > 0
    for t in y_to + x_to + [sibling]:
        greet(t)

    for j in range(3):

        @pl.when((x < 3) & (others[j] > zh))
        def _():
            greet(z_to[j])

    @pl.when(has_prev)
    def _():
        greet((me[0], prv * 2 + 1))

    @pl.when(has_next)
    def _():
        greet((me[0], nxt * 2))
        greet((me[0], nxt * 2 + 1))

    peers = 6 + jnp.where(x < 3, zh, 0) + jnp.where(has_prev, 1, 0) + jnp.where(has_next, 2, 0)
    pl.semaphore_wait(barrier, peers)

    for j in range(3):

        @pl.when((x < 3) & (others[j] < zh))
        def _():
            pl.semaphore_signal(ready.at[zh], inc=1, device_id=z_to[j], device_id_type=MESH)

    def z_copy(k, j, e, source):
        part = wb.at[k, rows_of(y, e, PART * jnp.minimum(x, 2), PART)]
        return remote(part, part, zs.at[k, j], zr.at[k, source], z_to[j])

    def x_copy(k, i, d, owner):
        part = wb.at[k, rows_of(y, i + 1, PART * jnp.minimum(owner, 2), PART)]
        return remote(part, part, xs.at[k, i, d], xr.at[k, i, d], x_to[d])

    def y_copy(k, e, d, yy):
        part = wb.at[k, rows_of(yy, e, 0, DEPTH)]
        return remote(part, part, ys.at[k, e, d], yr.at[k, e, d], y_to[d])

    def f_copy(k, e, d, yy):
        part = wb.at[k, rows_of(yy, e, HALF * d, HALF)]
        return remote(part, part, fs.at[k, e, d], fr.at[k, e, d], y_to[d])

    def z_down():
        for k in range(CHUNKS):
            for j in range(3):

                @pl.when((x < 3) & (others[j] < zh))
                def _():
                    z_copy(k, j, 0, zh).start()

    def z_up(j):
        @pl.when((x < 3) & (others[j] > zh))
        def _():
            pl.semaphore_wait(ready.at[others[j]], 1)
            z_copy(0, j, 0, zh).start()

    def z_more(k):
        for j in range(3):

            @pl.when((x < 3) & (others[j] > zh))
            def _():
                z_copy(k, j, 0, zh).start()

    def y_send(k, e):
        for d in range(2):
            y_copy(k, e, d, y).start()

    def z_to_x(k, j):
        @pl.when(x < 3)
        def _():
            z_copy(k, j, j + 1, others[j]).wait_recv()
            for d in range(3):
                x_copy(k, j, d, x).start()

    def x_to_y(k, j):
        for d in range(3):
            owner = (x + 3 - d) % 4

            @pl.when(owner < 3)
            def _():
                x_copy(k, j, d, owner).wait_recv()

        y_send(k, j + 1)

    def y_to_f(k, e):
        for d in range(2):
            yy = y + (3, 1)[d]
            y_copy(k, e, d, yy).wait_recv()
            f_copy(k, e, d, yy).start()

    def f_end(k, e):
        for d in range(2):
            f_copy(k, e, d, y + 2).wait_recv()

    def halo(i):
        return remote(
            x_hbm.at[0, pl.ds(STRETCH * (i + 1), STRETCH)], xb.at[pl.ds(STRETCH * i, STRETCH)],
            hs.at[i], hr.at[0], (me[0], nxt * 2 + i),
        )

    def halo_across(part_of):
        part = xb.at[pl.ds(pl.multiple_of(STRETCH * part_of, 16), STRETCH)]
        return remote(part, part, gs.at[0], gr.at[0], sibling)

    def to_sibling(rows):
        part = xb.at[pl.ds(pl.multiple_of(REACH + rows * ROWS, 16), ROWS)]
        return remote(x_hbm.at[0], part, cs.at[0], cr.at[0], sibling)

    for k in range(CHUNKS):
        for j in range(3):
            own_weights(k, j).wait()
        y_send(k, 0)
    z_down()
    to_sibling(core).start()

    @pl.when(has_next)
    def _():
        halo(0).start()
        halo(1).start()

    @pl.loop(0, 6)
    def _(b):
        block = chip * 6 + b
        owner = utt_ref[0, block]
        reach = left_ref[0, block]
        start = start_ref[0, owner]
        for d in (2, 1, 0):
            j = block - d
            ok = (j >= 0) & (utt_ref[0, jnp.maximum(j, 0)] == owner) & (reach >= d)
            pos = j * STRETCH + lax.broadcasted_iota(jnp.int32, (1, STRETCH), 1)
            first = jnp.where(ok, start, 1 << 30)
            at = STRETCH * (2 - d)
            masks[pl.ds(b, 1), at : at + STRETCH] = jnp.where(pos >= first, 0.0, -jnp.inf).astype(F32)

    @pl.when(jnp.logical_not(has_prev))
    def _():
        xb[0:REACH] = jnp.zeros((REACH, xb.shape[1]), BF16)

    def project(chunks):
        @pl.loop(0, CHIP // 512)
        def _(r):
            rr = pl.ds(pl.multiple_of(REACH + r * 512, 512), 512)
            weights = jnp.concatenate([wb[k] for k in chunks], axis=1)
            p = jnp.dot(xb[rr, :], weights, preferred_element_type=F32).astype(BF16)
            for n, k in enumerate(chunks):
                to = slice(k * 128, (k + 1) * 128)
                for j, ref in enumerate((qb, kb, vb)):
                    ref[rr, to] = p[:, n * 384 + j * 128 : n * 384 + j * 128 + 128]

    def project_halo():
        weights = jnp.concatenate([wb[k, :, 128:384] for k in range(CHUNKS)], axis=1)
        p = jnp.dot(xb[0:REACH, :], weights, preferred_element_type=F32).astype(BF16)
        for k in range(CHUNKS):
            kb[0:REACH, k * 128 : (k + 1) * 128] = p[:, k * 256 : k * 256 + 128]
            vb[0:REACH, k * 128 : (k + 1) * 128] = p[:, k * 256 + 128 : k * 256 + 256]

    lane = lax.broadcasted_iota(jnp.int32, (1, 128), 1)

    def window(h):
        t0, t1 = (h * HEAD_DIM) // 128, (h * HEAD_DIM + HEAD_DIM - 1) // 128
        low, width = h * HEAD_DIM - t0 * 128, (t1 - t0 + 1) * 128
        lanes = lax.broadcasted_iota(jnp.int32, (1, width), 1)
        return slice(t0 * 128, t0 * 128 + width), low, (lanes >= low) & (lanes < low + HEAD_DIM)

    def scores_of(h, b):
        cols, _, mine = window(h)
        rq = pl.ds(pl.multiple_of((b + 2) * STRETCH, STRETCH), STRETCH)
        rk = pl.ds(pl.multiple_of(b * STRETCH, STRETCH), 3 * STRETCH)
        q = jnp.where(mine, qb[rq, cols], jnp.zeros((), BF16))
        return lax.dot_general(q, kb[rk, cols], (((1,), (1,)), ((), ())), preferred_element_type=F32)

    def weights_of(s, bias):
        s = s + bias
        return jnp.exp2((s - jnp.max(s, axis=1, keepdims=True)) * SCALE).astype(BF16)

    def mixed_of(h, b, e, live):
        cols, low, mine = window(h)
        rk = pl.ds(pl.multiple_of(b * STRETCH, STRETCH), 3 * STRETCH)
        v = jnp.where(mine, vb[rk, cols], jnp.ones((), BF16))
        o = jnp.dot(e, v, preferred_element_type=F32)
        one = 0 if low > 0 else HEAD_DIM
        return jnp.where(live, o / o[:, one : one + 1], 0.0).astype(BF16)

    def block_of(b):
        block = chip * 6 + b
        start = start_ref[0, utt_ref[0, block]]
        live = block * STRETCH + lax.broadcasted_iota(jnp.int32, (STRETCH, 1), 0) >= start
        rr = pl.ds(pl.multiple_of(b * STRETCH, STRETCH), STRETCH)
        return live, rr, masks[pl.ds(b, 1), :]

    def out_parts(b, to):
        src = pl.ds(pl.multiple_of(b * STRETCH, STRETCH), STRETCH)
        ro = pl.ds(pl.multiple_of(to * STRETCH, STRETCH), STRETCH)
        return src, out_hbm.at[0, ro, pl.ds(pl.multiple_of(core * COLS, 128), COLS)]

    def attend():
        @pl.loop(0, 6)
        def _(step):
            blocks = [lax.rem(step * 1 + n + 3 * (1 - core), 6) for n in range(1)]
            heads = range(4)
            each = [block_of(b) for b in blocks]
            scores = [[scores_of(h, b) for h in heads] for b in blocks]
            shares = [[weights_of(s, each[n][2]) for s in scores[n]] for n in range(1)]
            for n, b in enumerate(blocks):
                live, rr, _ = each[n]
                o = [mixed_of(h, b, shares[n][h], live) for h in heads]
                ob[rr, 0:128] = jnp.where(lane < 96, o[0], o[1][:, :128])
                ob[rr, 128:256] = jnp.where(lane < 64, o[1][:, 128:], o[2][:, :128])
                ob[rr, 256:384] = jnp.where(lane < 32, o[2][:, 128:], o[3])
                i = lax.rem(b, 3)
                src, dst = out_parts(b, i)
                here = (b // 3) == core

                @pl.when(here)
                def _(src=src, dst=dst, i=i):
                    pltpu.make_async_copy(ob.at[src], dst, lo.at[i]).start()

                @pl.when(jnp.logical_not(here))
                def _(src=src, dst=dst, i=i):
                    remote(ob.at[src], dst, os_.at[i], or_.at[i], sibling).start()

    z_up(0)
    for k in range(CHUNKS):
        y_to_f(k, 0)
    z_up(1)
    z_up(2)
    z_to_x(0, 0)
    z_to_x(0, 1)
    z_more(1)
    x_to_y(0, 0)
    x_to_y(0, 1)
    z_to_x(0, 2)
    z_to_x(1, 0)
    z_to_x(1, 1)
    z_more(2)
    x_to_y(0, 2)
    x_to_y(1, 0)
    x_to_y(1, 1)
    y_to_f(0, 1)
    y_to_f(0, 2)
    z_to_x(1, 2)
    z_to_x(2, 0)
    z_to_x(2, 1)
    x_to_y(1, 2)
    x_to_y(2, 0)
    x_to_y(2, 1)
    y_to_f(0, 3)
    y_to_f(1, 1)
    y_to_f(1, 2)
    z_to_x(2, 2)
    own_frames.wait()
    to_sibling(1 - core).wait_recv()
    y_to_f(1, 3)
    x_to_y(2, 2)
    y_to_f(2, 1)
    y_to_f(2, 2)

    @pl.when(has_prev)
    def _():
        part = xb.at[pl.ds(pl.multiple_of(STRETCH * core, 16), STRETCH)]
        remote(part, part, gs.at[0], hr.at[0], sibling).wait_recv()
        halo_across(core).start()

    y_to_f(2, 3)

    for k in range(2):
        for e in range(4):
            f_end(k, e)
    project((0, 1))

    @pl.when(has_prev)
    def _():
        halo_across(1 - core).wait_recv()

    for e in range(4):
        f_end(2, e)
    project((2,))
    project_halo()
    attend()

    for i in range(3):
        src, dst = out_parts(i, i)
        pltpu.make_async_copy(ob.at[src], dst, lo.at[i]).wait()
        other = out_hbm.at[0, pl.ds(i * STRETCH, STRETCH), pl.ds(pl.multiple_of((1 - core) * COLS, 128), COLS)]
        c = remote(ob.at[src], other, os_.at[i], or_.at[i], sibling)
        c.wait_send()
        c.wait_recv()
    for k in range(CHUNKS):
        for e in range(4):
            for d in range(2):
                y_copy(k, e, d, y).wait_send()
                f_copy(k, e, d, y).wait_send()

        @pl.when(x < 3)
        def _():
            for i in range(3):
                z_copy(k, i, 0, zh).wait_send()
                for d in range(3):
                    x_copy(k, i, d, x).wait_send()

    to_sibling(core).wait_send()

    @pl.when(has_next)
    def _():
        halo(0).wait_send()
        halo(1).wait_send()

    @pl.when(has_prev)
    def _():
        halo_across(core).wait_send()


def local(frames, w_qkv, utt_start, stretch_utt, left_stretches):
    any_ = pl.BlockSpec(memory_space=pl.ANY)
    smem = pl.BlockSpec(memory_space=pltpu.SMEM)
    dma = pltpu.SemaphoreType.DMA
    return pl.pallas_call(
        kernel,
        out_shape=jax.ShapeDtypeStruct((1, ROWS, 768), BF16),
        in_specs=[any_, any_, smem, smem, smem],
        out_specs=any_,
        scratch_shapes=[
            pltpu.VMEM((REACH + CHIP, 1536), BF16),
            pltpu.VMEM((CHUNKS, 1536, COLS), BF16),
            pltpu.VMEM((REACH + CHIP, COLS), BF16),
            pltpu.VMEM((REACH + CHIP, COLS), BF16),
            pltpu.VMEM((REACH + CHIP, COLS), BF16),
            pltpu.VMEM((CHIP, COLS), BF16),
            pltpu.VMEM((8, 3 * STRETCH), F32),
            dma((1,)), dma((CHUNKS, 3)),
            dma((1,)), dma((1,)), dma((2,)), dma((1,)), dma((1,)), dma((1,)),
            dma((CHUNKS, 3)), dma((CHUNKS, 4)), dma((CHUNKS, 3, 3)), dma((CHUNKS, 3, 3)),
            dma((CHUNKS, 4, 2)), dma((CHUNKS, 4, 2)), dma((CHUNKS, 4, 2)), dma((CHUNKS, 4, 2)),
            dma((3,)), dma((3,)), dma((3,)),
            pltpu.SemaphoreType.REGULAR((4,)),
        ],
        compiler_params=pltpu.CompilerParams(
            collective_id=0, has_side_effects=True, vmem_limit_bytes=60 << 20
        ),
        name="block_attention",
    )(frames, w_qkv, utt_start, stretch_utt, left_stretches)


def solution(mesh):
    return jax.shard_map(
        local,
        mesh=mesh,
        in_specs=(P("dp", "tm", None), P("dp", None), P("dp", None), P("dp", None), P("dp", None)),
        out_specs=P("dp", "tm", None),
        check_vma=False,
    )
```

```python
import functools

import jax
import jax.numpy as jnp
from jax import lax
from jax.experimental import pallas as pl
from jax.experimental.pallas import tpu as pltpu
from jax.sharding import PartitionSpec as P

MESH = pl.DeviceIdType.MESH
BF16, F32 = jnp.bfloat16, jnp.float32
HEAD_DIM = 96
STRETCH = 256
ROWS = 768
CHIP = 1536
REACH = 512
DEPTH = 96
HALF = 48
PART = 32
COLS = 384
CHUNKS = 3
SCALE = HEAD_DIM**-0.5 * 1.4426950408889634


def place():
    dp, tm = lax.axis_index("dp"), lax.axis_index("tm")
    return dp // 4, dp % 4, tm // 8, (tm // 2) % 4, tm % 2


def device(y, z, x, core):
    y, z, x = (y + 4) % 4, (z + 16) % 16, (x + 4) % 4
    return (y * 4 + z // 4, (z % 4) * 8 + x * 2 + core)


def remote(src, dst, send, recv, target):
    return pltpu.make_async_remote_copy(
        src_ref=src, dst_ref=dst, send_sem=send, recv_sem=recv, device_id=target, device_id_type=MESH
    )


def kernel(
    x_hbm, w_hbm, start_ref, utt_ref, left_ref, out_hbm,
    xb, wb, qb, kb, vb, ob, masks,
    lx, lw, cs, cr, hs, hr, gs, gr, zs, zr, xs, xr, ys, yr, fs, fr, os_, or_, lo, ready,
):
    y, zh, zl, x, core = place()
    z = zh * 4 + zl
    me = device(y, z, x, core)
    sibling = (me[0], me[1] + 1 - 2 * core)
    y_to = [device(y + 1, z, x, core), device(y + 3, z, x, core)]
    others = [jnp.where(zh == 3, 2 - j, j + jnp.where(j >= zh, 1, 0)) for j in range(3)]
    z_to = [device(y, o * 4 + zl, x, core) for o in others]
    x_to = [device(y, z, x + d, core) for d in (1, 2, 3)]
    groups = [zh] + others
    chip = me[1] // 2
    nxt, prv = (chip + 1) % 16, (chip + 15) % 16

    def rows_of(yy, e, start, count):
        first = ((yy + 4) % 4 * 4 + groups[e]) * DEPTH + start
        return pl.ds(pl.multiple_of(first, 16), count)

    barrier = pltpu.get_barrier_semaphore()

    def greet(target):
        pl.semaphore_signal(barrier, inc=1, device_id=target, device_id_type=MESH)

    own_rows = rows_of(y, 0, 0, DEPTH)

    def own_weights(k, j):
        col = pl.multiple_of(j * 768 + core * 384 + k * 128, 128)
        return pltpu.make_async_copy(
            w_hbm.at[:, pl.ds(col, 128)], wb.at[k, own_rows, pl.ds(j * 128, 128)], lw.at[k, j]
        )

    for k in range(CHUNKS):
        for j in range(3):
            own_weights(k, j).start()
    own_x = pl.ds(pl.multiple_of(REACH + core * ROWS, 16), ROWS)
    own_frames = pltpu.make_async_copy(x_hbm.at[0], xb.at[own_x], lx.at[0])
    own_frames.start()

    has_next = (core == 1) & (chip < 15)
    has_prev = chip > 0
    for t in y_to + x_to + [sibling]:
        greet(t)

    for j in range(3):

        @pl.when((x < 3) & (others[j] > zh))
        def _():
            greet(z_to[j])

    @pl.when(has_prev)
    def _():
        greet((me[0], prv * 2 + 1))

    @pl.when(has_next)
    def _():
        greet((me[0], nxt * 2))
        greet((me[0], nxt * 2 + 1))

    peers = 6 + jnp.where(x < 3, zh, 0) + jnp.where(has_prev, 1, 0) + jnp.where(has_next, 2, 0)
    pl.semaphore_wait(barrier, peers)

    for j in range(3):

        @pl.when((x < 3) & (others[j] < zh))
        def _():
            pl.semaphore_signal(ready.at[zh], inc=1, device_id=z_to[j], device_id_type=MESH)

    def z_copy(k, j, e, source):
        part = wb.at[k, rows_of(y, e, PART * jnp.minimum(x, 2), PART)]
        return remote(part, part, zs.at[k, j], zr.at[k, source], z_to[j])

    def x_copy(k, i, d, owner):
        part = wb.at[k, rows_of(y, i + 1, PART * jnp.minimum(owner, 2), PART)]
        return remote(part, part, xs.at[k, i, d], xr.at[k, i, d], x_to[d])

    def y_copy(k, e, d, yy):
        part = wb.at[k, rows_of(yy, e, 0, DEPTH)]
        return remote(part, part, ys.at[k, e, d], yr.at[k, e, d], y_to[d])

    def f_copy(k, e, d, yy):
        part = wb.at[k, rows_of(yy, e, HALF * d, HALF)]
        return remote(part, part, fs.at[k, e, d], fr.at[k, e, d], y_to[d])

    def z_down():
        for k in range(CHUNKS):
            for j in (2, 1, 0):

                @pl.when((x < 3) & (others[j] < zh))
                def _():
                    z_copy(k, j, 0, zh).start()

    def z_up(j):
        @pl.when((x < 3) & (others[j] > zh))
        def _():
            pl.semaphore_wait(ready.at[others[j]], 1)
            z_copy(0, j, 0, zh).start()

    def z_more(k):
        for j in range(3):

            @pl.when((x < 3) & (others[j] > zh))
            def _():
                z_copy(k, j, 0, zh).start()

    def y_send(k, e):
        for d in range(2):
            y_copy(k, e, d, y).start()

    def z_to_x(k, j):
        @pl.when(x < 3)
        def _():
            z_copy(k, j, j + 1, others[j]).wait_recv()
            for d in range(3):
                x_copy(k, j, d, x).start()

    def x_to_y(k, j):
        for d in range(3):
            owner = (x + 3 - d) % 4

            @pl.when(owner < 3)
            def _():
                x_copy(k, j, d, owner).wait_recv()

        y_send(k, j + 1)

    def y_to_f(k, e):
        for d in range(2):
            yy = y + (3, 1)[d]
            y_copy(k, e, d, yy).wait_recv()
            f_copy(k, e, d, yy).start()

    def f_end(k, e):
        for d in range(2):
            f_copy(k, e, d, y + 2).wait_recv()

    def halo(i):
        return remote(
            x_hbm.at[0, pl.ds(STRETCH * (i + 1), STRETCH)], xb.at[pl.ds(STRETCH * i, STRETCH)],
            hs.at[i], hr.at[0], (me[0], nxt * 2 + i),
        )

    def halo_across(part_of):
        part = xb.at[pl.ds(pl.multiple_of(STRETCH * part_of, 16), STRETCH)]
        return remote(part, part, gs.at[0], gr.at[0], sibling)

    def to_sibling(rows):
        part = xb.at[pl.ds(pl.multiple_of(REACH + rows * ROWS, 16), ROWS)]
        return remote(x_hbm.at[0], part, cs.at[0], cr.at[0], sibling)

    for k in range(CHUNKS):
        for j in range(3):
            own_weights(k, j).wait()
        y_send(k, 0)
    z_down()
    to_sibling(core).start()

    @pl.when(has_next)
    def _():
        halo(0).start()
        halo(1).start()

    @pl.loop(0, 6)
    def _(b):
        block = chip * 6 + b
        owner = utt_ref[0, block]
        reach = left_ref[0, block]
        start = start_ref[0, owner]
        for d in (2, 1, 0):
            j = block - d
            ok = (j >= 0) & (utt_ref[0, jnp.maximum(j, 0)] == owner) & (reach >= d)
            pos = j * STRETCH + lax.broadcasted_iota(jnp.int32, (1, STRETCH), 1)
            first = jnp.where(ok, start, 1 << 30)
            at = STRETCH * (2 - d)
            masks[pl.ds(b, 1), at : at + STRETCH] = jnp.where(pos >= first, 0.0, -jnp.inf).astype(F32)

    @pl.when(jnp.logical_not(has_prev))
    def _():
        xb[0:REACH] = jnp.zeros((REACH, xb.shape[1]), BF16)

    def project(chunks):
        @pl.loop(0, CHIP // 512)
        def _(r):
            rr = pl.ds(pl.multiple_of(REACH + r * 512, 512), 512)
            weights = jnp.concatenate([wb[k] for k in chunks], axis=1)
            p = jnp.dot(xb[rr, :], weights, preferred_element_type=F32).astype(BF16)
            for n, k in enumerate(chunks):
                to = slice(k * 128, (k + 1) * 128)
                for j, ref in enumerate((qb, kb, vb)):
                    ref[rr, to] = p[:, n * 384 + j * 128 : n * 384 + j * 128 + 128]

    def project_halo():
        weights = jnp.concatenate([wb[k, :, 128:384] for k in range(CHUNKS)], axis=1)
        p = jnp.dot(xb[0:REACH, :], weights, preferred_element_type=F32).astype(BF16)
        for k in range(CHUNKS):
            kb[0:REACH, k * 128 : (k + 1) * 128] = p[:, k * 256 : k * 256 + 128]
            vb[0:REACH, k * 128 : (k + 1) * 128] = p[:, k * 256 + 128 : k * 256 + 256]

    lane = lax.broadcasted_iota(jnp.int32, (1, 128), 1)

    def window(h):
        t0, t1 = (h * HEAD_DIM) // 128, (h * HEAD_DIM + HEAD_DIM - 1) // 128
        low, width = h * HEAD_DIM - t0 * 128, (t1 - t0 + 1) * 128
        lanes = lax.broadcasted_iota(jnp.int32, (1, width), 1)
        return slice(t0 * 128, t0 * 128 + width), low, (lanes >= low) & (lanes < low + HEAD_DIM)

    def scores_of(h, b):
        cols, _, mine = window(h)
        rq = pl.ds(pl.multiple_of((b + 2) * STRETCH, STRETCH), STRETCH)
        rk = pl.ds(pl.multiple_of(b * STRETCH, STRETCH), 3 * STRETCH)
        q = jnp.where(mine, qb[rq, cols], jnp.zeros((), BF16))
        return lax.dot_general(q, kb[rk, cols], (((1,), (1,)), ((), ())), preferred_element_type=F32)

    def weights_of(s, bias):
        s = s + bias
        return jnp.exp2((s - jnp.max(s, axis=1, keepdims=True)) * SCALE).astype(BF16)

    def mixed_of(h, b, e, live):
        cols, low, mine = window(h)
        rk = pl.ds(pl.multiple_of(b * STRETCH, STRETCH), 3 * STRETCH)
        v = jnp.where(mine, vb[rk, cols], jnp.ones((), BF16))
        o = jnp.dot(e, v, preferred_element_type=F32)
        one = 0 if low > 0 else HEAD_DIM
        return jnp.where(live, o / o[:, one : one + 1], 0.0).astype(BF16)

    def block_of(b):
        block = chip * 6 + b
        start = start_ref[0, utt_ref[0, block]]
        live = block * STRETCH + lax.broadcasted_iota(jnp.int32, (STRETCH, 1), 0) >= start
        rr = pl.ds(pl.multiple_of(b * STRETCH, STRETCH), STRETCH)
        return live, rr, masks[pl.ds(b, 1), :]

    def out_parts(b, to):
        src = pl.ds(pl.multiple_of(b * STRETCH, STRETCH), STRETCH)
        ro = pl.ds(pl.multiple_of(to * STRETCH, STRETCH), STRETCH)
        return src, out_hbm.at[0, ro, pl.ds(pl.multiple_of(core * COLS, 128), COLS)]

    def attend():
        @pl.loop(0, 6)
        def _(step):
            blocks = [lax.rem(step * 1 + n + 3 * (1 - core), 6) for n in range(1)]
            heads = range(4)
            each = [block_of(b) for b in blocks]
            scores = [[scores_of(h, b) for h in heads] for b in blocks]
            shares = [[weights_of(s, each[n][2]) for s in scores[n]] for n in range(1)]
            for n, b in enumerate(blocks):
                live, rr, _ = each[n]
                o = [mixed_of(h, b, shares[n][h], live) for h in heads]
                ob[rr, 0:128] = jnp.where(lane < 96, o[0], o[1][:, :128])
                ob[rr, 128:256] = jnp.where(lane < 64, o[1][:, 128:], o[2][:, :128])
                ob[rr, 256:384] = jnp.where(lane < 32, o[2][:, 128:], o[3])
                i = lax.rem(b, 3)
                src, dst = out_parts(b, i)
                here = (b // 3) == core

                @pl.when(here)
                def _(src=src, dst=dst, i=i):
                    pltpu.make_async_copy(ob.at[src], dst, lo.at[i]).start()

                @pl.when(jnp.logical_not(here))
                def _(src=src, dst=dst, i=i):
                    remote(ob.at[src], dst, os_.at[i], or_.at[i], sibling).start()

    z_up(0)
    for k in range(CHUNKS):
        y_to_f(k, 0)
    z_up(1)
    z_up(2)
    z_to_x(0, 0)
    z_to_x(0, 1)
    z_more(1)
    x_to_y(0, 0)
    x_to_y(0, 1)
    z_to_x(0, 2)
    z_to_x(1, 0)
    z_to_x(1, 1)
    z_more(2)
    x_to_y(0, 2)
    x_to_y(1, 0)
    x_to_y(1, 1)
    y_to_f(0, 1)
    y_to_f(0, 2)
    z_to_x(1, 2)
    z_to_x(2, 0)
    z_to_x(2, 1)
    x_to_y(1, 2)
    x_to_y(2, 0)
    x_to_y(2, 1)
    y_to_f(0, 3)
    y_to_f(1, 1)
    y_to_f(1, 2)
    z_to_x(2, 2)
    own_frames.wait()
    to_sibling(1 - core).wait_recv()
    y_to_f(1, 3)
    x_to_y(2, 2)
    y_to_f(2, 1)
    y_to_f(2, 2)

    @pl.when(has_prev)
    def _():
        part = xb.at[pl.ds(pl.multiple_of(STRETCH * core, 16), STRETCH)]
        remote(part, part, gs.at[0], hr.at[0], sibling).wait_recv()
        halo_across(core).start()

    y_to_f(2, 3)

    for k in range(2):
        for e in range(4):
            f_end(k, e)
    project((0, 1))

    @pl.when(has_prev)
    def _():
        halo_across(1 - core).wait_recv()

    for e in range(4):
        f_end(2, e)
    project((2,))
    project_halo()
    attend()

    for i in range(3):
        src, dst = out_parts(i, i)
        pltpu.make_async_copy(ob.at[src], dst, lo.at[i]).wait()
        other = out_hbm.at[0, pl.ds(i * STRETCH, STRETCH), pl.ds(pl.multiple_of((1 - core) * COLS, 128), COLS)]
        c = remote(ob.at[src], other, os_.at[i], or_.at[i], sibling)
        c.wait_send()
        c.wait_recv()
    for k in range(CHUNKS):
        for e in range(4):
            for d in range(2):
                y_copy(k, e, d, y).wait_send()
                f_copy(k, e, d, y).wait_send()

        @pl.when(x < 3)
        def _():
            for i in range(3):
                z_copy(k, i, 0, zh).wait_send()
                for d in range(3):
                    x_copy(k, i, d, x).wait_send()

    to_sibling(core).wait_send()

    @pl.when(has_next)
    def _():
        halo(0).wait_send()
        halo(1).wait_send()

    @pl.when(has_prev)
    def _():
        halo_across(core).wait_send()


def local(frames, w_qkv, utt_start, stretch_utt, left_stretches):
    any_ = pl.BlockSpec(memory_space=pl.ANY)
    smem = pl.BlockSpec(memory_space=pltpu.SMEM)
    dma = pltpu.SemaphoreType.DMA
    return pl.pallas_call(
        kernel,
        out_shape=jax.ShapeDtypeStruct((1, ROWS, 768), BF16),
        in_specs=[any_, any_, smem, smem, smem],
        out_specs=any_,
        scratch_shapes=[
            pltpu.VMEM((REACH + CHIP, 1536), BF16),
            pltpu.VMEM((CHUNKS, 1536, COLS), BF16),
            pltpu.VMEM((REACH + CHIP, COLS), BF16),
            pltpu.VMEM((REACH + CHIP, COLS), BF16),
            pltpu.VMEM((REACH + CHIP, COLS), BF16),
            pltpu.VMEM((CHIP, COLS), BF16),
            pltpu.VMEM((8, 3 * STRETCH), F32),
            dma((1,)), dma((CHUNKS, 3)),
            dma((1,)), dma((1,)), dma((2,)), dma((1,)), dma((1,)), dma((1,)),
            dma((CHUNKS, 3)), dma((CHUNKS, 4)), dma((CHUNKS, 3, 3)), dma((CHUNKS, 3, 3)),
            dma((CHUNKS, 4, 2)), dma((CHUNKS, 4, 2)), dma((CHUNKS, 4, 2)), dma((CHUNKS, 4, 2)),
            dma((3,)), dma((3,)), dma((3,)),
            pltpu.SemaphoreType.REGULAR((4,)),
        ],
        compiler_params=pltpu.CompilerParams(
            collective_id=0, has_side_effects=True, vmem_limit_bytes=60 << 20
        ),
        name="block_attention",
    )(frames, w_qkv, utt_start, stretch_utt, left_stretches)


def solution(mesh):
    return jax.shard_map(
        local,
        mesh=mesh,
        in_specs=(P("dp", "tm", None), P("dp", None), P("dp", None), P("dp", None), P("dp", None)),
        out_specs=P("dp", "tm", None),
        check_vma=False,
    )
```
